512 devices in a mesh: frames: 128 (over z, y, x_lo), heads: 4 (over x_hi, core).
Axes of the slice: x: 4 (x_hi: 2, x_lo: 2; x = x_hi * 2 + x_lo), y: 8, z: 8, core: 2. Of those that a mesh axis runs over, the one named last changes fastest.
Arguments:
- queries: bfloat16 [12288, 2560], P('frames', 'heads'), may hold values from -40 to 40
- keys_values: bfloat16 [2, 12288, 2560], P(None, 'frames', 'heads'), may hold values from -40 to 40
- out_weight: bfloat16 [2560, 5120], P('heads', 'frames'), may hold values from -0.5 to 0.5
Outputs:
- projected: bfloat16 [12288, 5120], P('frames', 'heads')
The draws below stay inside these ranges and needn't reach their ends.
All inputs are finite; a program needn't handle non-finite values.
Results may differ from the reference program's by a relative error of at most 0.015.
Values may be sent and summed in bfloat16 or wider, within the bound.
A program may use at most 64 MiB of HBM per device.

```python
import math
import jax
import jax.numpy as jnp
from jax import lax

D = 5120
HD = 128
HEADS = 20
TPF = 32
FRAMES = 384
BAND = 32
TOKENS = 12288


def shared_fields(key):
    base = jax.random.fold_in(key, 11)
    first, second, third = jax.random.split(base, 3)
    shape = (TOKENS, HEADS * HD)
    scale = jnp.exp(jax.random.uniform(third, (TOKENS, 1), jnp.float32, math.log(0.25), math.log(2.5)))
    keys = jnp.clip(jax.random.normal(first, shape, jnp.float32), -6.0, 6.0) * scale
    queries = jnp.clip(jax.random.normal(second, shape, jnp.float32), -6.0, 6.0)
    return (queries, keys)


def draw_queries(key, part):
    queries, keys = shared_fields(key)
    return queries.astype(jnp.bfloat16)


def draw_keys_values(key, part):
    queries, keys = shared_fields(key)
    value_key = jax.random.fold_in(key, 23)
    values = jnp.clip(jax.random.normal(value_key, (TOKENS, HEADS * HD), jnp.float32), -6.0, 6.0)
    return jnp.stack([keys, values]).astype(jnp.bfloat16)


def block_levels(rng, shape, shards, smallest, largest):
    def one(position, blocks):
        draws = jax.random.uniform(jax.random.fold_in(jax.random.fold_in(rng, 6), position), (blocks,), jnp.float32, smallest / len(shards), largest / len(shards))
        return jnp.repeat(jnp.exp(draws), shape[position] // blocks).reshape((-1,) + (1,) * (len(shape) - position - 1))

    factor_of = one(*shards[0])
    for cut in shards[1:]:
        factor_of = factor_of * one(*cut)
    return factor_of


def scatter_about(rng, shape, spread, limit, pieces=(), held_as=jnp.bfloat16):
    result = jax.random.normal(rng, shape, jnp.float32) * spread
    if len(pieces) > 0:
        result = block_levels(rng, shape, pieces, -0.22, 0.18) * result
    return jnp.clip(result, min=-limit, max=limit).astype(held_as)


def setup_inputs(seed: int = 0) -> dict:
    seeds = jax.random.split(jax.random.key(seed), 4)
    return {
        "queries": draw_queries(jax.random.fold_in(seeds[3], 71), 0),
        "keys_values": draw_keys_values(jax.random.fold_in(seeds[3], 71), 0),
        "out_weight": scatter_about(seeds[2], (HEADS * HD, D), HD ** -0.5, 0.5, ((0, 4), (1, 128))),
    }


def reference(queries, keys_values, out_weight):
    query_frames = queries.reshape(FRAMES, TPF, HEADS, HD)
    key_frames = keys_values[0].reshape(FRAMES, TPF, HEADS, HD)
    value_frames = keys_values[1].reshape(FRAMES, TPF, HEADS, HD)
    offsets = jnp.arange(2 * BAND + 1, dtype=jnp.int32) - BAND

    def one_frame(frame):
        picks = ((frame + offsets) % FRAMES).astype(jnp.int32)
        keys = key_frames[picks].reshape((2 * BAND + 1) * TPF, HEADS, HD).astype(jnp.float32)
        values = value_frames[picks].reshape((2 * BAND + 1) * TPF, HEADS, HD).astype(jnp.float32)
        query = query_frames[frame].astype(jnp.float32)
        scores = jnp.einsum("qhd,khd->hqk", query, keys, precision=lax.Precision.HIGHEST)
        scores = scores * (HD ** -0.5)
        top = jnp.max(scores, axis=2, keepdims=True)
        weights = jnp.exp(scores - top)
        probs = (weights / jnp.sum(weights, axis=2, keepdims=True)).astype(jnp.bfloat16)
        attended = jnp.einsum("hqk,khd->qhd", probs.astype(jnp.float32), values, precision=lax.Precision.HIGHEST)
        return attended.astype(jnp.bfloat16).reshape(TPF, HEADS * HD)

    attended = lax.map(one_frame, jnp.arange(FRAMES, dtype=jnp.int32)).reshape(TOKENS, HEADS * HD)
    return jnp.dot(attended, out_weight, preferred_element_type=jnp.float32).astype(jnp.bfloat16)
```

```python
import jax
import jax.numpy as jnp
from jax import lax
from jax.experimental import pallas as pl
from jax.experimental.pallas import tpu as pltpu
from jax.sharding import PartitionSpec as P

HD = 128
TPF = 32
NY = 8
NZ = 8
LOCAL_HEADS = 5
ROWS = 96
UNIT = 768
WINDOW = 2816
SUB = 256
KEYS = 2304
COLS = 40
PADDED = 48
KA = 256
KB = 384
NEG = -1e30
LOGE = 1.4426950408889634
MESH = pl.DeviceIdType.MESH


def on_core(q_ref, kv_ref, w_ref, out_ref,
            kv_win, q_win, o_buf, scores, a_buf, wa, wb, part, c_in, summed, x_in, spread,
            p1_s, kv_r, q_r, h_s, h_r, w1_s, w1_r, w2_s, w2_r, o_s, o_r, c_s, c_r, x_s, x_r):
    frames = lax.axis_index("frames")
    heads = lax.axis_index("heads")
    xl = lax.rem(frames, 2)
    y = lax.rem(lax.div(frames, 2), NY)
    z = lax.div(frames, 2 * NY)
    xh = lax.div(heads, 2)
    core = lax.rem(heads, 2)

    def dev(zz, yy, xx, hh, cc):
        return ((zz * NY + yy) * 2 + xx, hh * 2 + cc)

    def remote(src, dst, send, recv, device):
        return pltpu.make_async_remote_copy(
            src_ref=src, dst_ref=dst, send_sem=send, recv_sem=recv,
            device_id=device, device_id_type=MESH)

    mine = (y * 2 + xl) * 2 + core
    partner = dev(z, y, xl, xh, 1 - core)
    barrier = pltpu.get_barrier_semaphore()

    def greet(device):
        pl.semaphore_signal(barrier, inc=1, device_id=device, device_id_type=MESH)

    for k in range(1, 32):
        other = lax.rem(mine + k, 32)
        greet(dev(z, lax.div(other, 4), lax.rem(lax.div(other, 2), 2), xh, lax.rem(other, 2)))
    for k in range(1, NZ):
        greet(dev(lax.rem(z + k, NZ), y, xl, xh, core))
    for k in (1, NZ - 1):
        greet(dev(lax.rem(z + k, NZ), y, xl, xh, 1 - core))
    for k in (0, 1):
        greet(dev(z, y, k, 1 - xh, core))
    pl.semaphore_wait(barrier, 31 + 7 + 2 + 2)

    slot = lax.rem(y, 4) * 2 + xl
    dest_core = lax.div(y, 4)
    selves = []
    for a in range(LOCAL_HEADS):
        place = lax.div((core * LOCAL_HEADS + a) * 8, 5)
        yd, xd = lax.div(place, 2), lax.rem(place, 2)
        to_self = (yd == y) & (xd == xl) & (dest_core == core)
        selves.append(to_self)
        target = dev(z, yd, xd, xh, dest_core)
        kv_src = kv_ref.at[:, :, pl.ds(a * HD, HD)]
        q_src = q_ref.at[:, pl.ds(a * HD, HD)]
        kv_dst = kv_win.at[:, pl.ds(pl.multiple_of(1024 + slot * ROWS, 32), ROWS), :]
        q_dst = q_win.at[pl.ds(pl.multiple_of(slot * ROWS, 32), ROWS), :]

        @pl.when(to_self)
        def _():
            pltpu.make_async_copy(kv_src, kv_dst, kv_r.at[slot]).start()
            pltpu.make_async_copy(q_src, q_dst, q_r.at[slot]).start()

        @pl.when(jnp.logical_not(to_self))
        def _():
            remote(kv_src, kv_dst, p1_s.at[a], kv_r.at[slot], target).start()
            remote(q_src, q_dst, p1_s.at[LOCAL_HEADS + a], q_r.at[slot], target).start()

    wa[z, y] = w_ref[:, :KA]
    wb[z, y] = w_ref[:, KA:]
    for k in range(1, NZ):
        remote(wa.at[z, y], wa.at[z, y], w1_s.at[k - 1], w1_r.at[k - 1],
               dev(lax.rem(z + k, NZ), y, xl, xh, core)).start()
        remote(wb.at[z, y], wb.at[z, y], w1_s.at[6 + k], w1_r.at[6 + k],
               dev(z, lax.rem(y + k, NY), xl, xh, core)).start()

    place = y * 2 + xl
    head = lax.div(place * 5 + 7, 8)
    active = lax.div(head * 8, 5) == place
    unit = z * 2 + core

    def unit_dev(shift):
        other = lax.rem(unit + shift + 16, 16)
        return dev(lax.div(other, 2), y, xl, xh, lax.rem(other, 2))

    halos = (
        (1024, UNIT, 256, 1),
        (1024, UNIT, 1792, -1),
        (1536, 256, 0, 2),
        (1024, 256, 2560, -2),
    )

    def halo(i):
        start, size, to, shift = halos[i]
        return remote(kv_win.at[:, pl.ds(start, size), :], kv_win.at[:, pl.ds(to, size), :],
                      h_s.at[i], h_r.at[i], unit_dev(shift))

    @pl.when(active)
    def _():
        for j in range(8):
            remote(kv_win.at[:, pl.ds(1024 + j * ROWS, ROWS), :],
                   kv_win.at[:, pl.ds(1024 + j * ROWS, ROWS), :],
                   kv_r.at[j], kv_r.at[j], partner).wait_recv()
        for i in range(4):
            halo(i).start()

    sign = 1 - 2 * core

    def ring(i):
        along_y = i < 7
        t = i if along_y else i - 7
        long = t < 4
        t = t if long else t - 4
        way = sign if long else -sign
        if along_y:
            block = lax.rem(y - way * t + 2 * NY, NY)
            target = dev(z, lax.rem(y + way + NY, NY), xl, xh, core)
            ref = wa.at[:, block]
        else:
            block = lax.rem(z - way * t + 2 * NZ, NZ)
            target = dev(lax.rem(z + way + NZ, NZ), y, xl, xh, core)
            ref = wb.at[block]
        return remote(ref, ref, w2_s.at[i], w2_r.at[i], target)

    def ring_arrival(i):
        along_y = i < 7
        t = i if along_y else i - 7
        long = t < 4
        t = t if long else t - 4
        way = sign if long else -sign
        if along_y:
            ref = wa.at[:, lax.rem(y - way * (t + 1) + 2 * NY, NY)]
        else:
            ref = wb.at[lax.rem(z - way * (t + 1) + 2 * NZ, NZ)]
        remote(ref, ref, w2_r.at[i], w2_r.at[i], partner).wait_recv()

    for k in range(1, NZ):
        back = lax.rem(z - k + NZ, NZ)
        remote(wa.at[back, y], wa.at[back, y], w1_r.at[k - 1], w1_r.at[k - 1], partner).wait_recv()
    ring(0).start()
    ring(4).start()
    for k in range(1, NY):
        back = lax.rem(y - k + NY, NY)
        remote(wb.at[z, back], wb.at[z, back], w1_r.at[6 + k], w1_r.at[6 + k], partner).wait_recv()
    ring(7).start()
    ring(11).start()

    def ring_step(t):
        for first, last in ((0, 3), (4, 6), (7, 10), (11, 13)):
            i = first + t
            if i < last:
                ring_arrival(i)
                ring(i + 1).start()
            elif i == last:
                ring_arrival(i)

    def attend(s):
        queries = q_win[pl.ds(s * SUB, SUB), :]
        top = jnp.full((SUB, 256), NEG, jnp.float32)
        rows = lax.broadcasted_iota(jnp.int32, (SUB, 256), 0) // TPF
        cols = lax.broadcasted_iota(jnp.int32, (SUB, 256), 1) // TPF
        for n in range(KEYS // 256):
            keys = kv_win[0, pl.ds(s * SUB + n * 256, 256), :]
            block = lax.dot_general(queries, keys, (((1,), (1,)), ((), ())),
                                    preferred_element_type=jnp.float32)
            if n == 0:
                block = jnp.where(cols >= rows, block, NEG)
            elif n == KEYS // 256 - 1:
                block = jnp.where(cols <= rows, block, NEG)
            scores[:, pl.ds(n * 256, 256)] = block
            top = jnp.maximum(top, block)
        peak = jnp.max(top, axis=1, keepdims=True)
        total = jnp.zeros((SUB, 256), jnp.float32)
        acc = jnp.zeros((SUB, HD), jnp.float32)
        for n in range(KEYS // 256):
            weights = jnp.exp2((scores[:, pl.ds(n * 256, 256)] - peak) * (LOGE * HD ** -0.5))
            total = total + weights
            values = kv_win[1, pl.ds(s * SUB + n * 256, 256), :]
            acc = acc + jnp.dot(weights.astype(jnp.bfloat16), values,
                                preferred_element_type=jnp.float32)
        norm = jnp.sum(total, axis=1, keepdims=True)
        o_buf[pl.ds(s * SUB, SUB), :] = (acc / norm).astype(jnp.bfloat16)

    home_core = lax.div(head, LOCAL_HEADS)
    home_head = lax.rem(head, LOCAL_HEADS)

    def home(r, xx):
        yy = core * 4 + r
        own = (yy == y) & (xx == xl) & (home_core == core)
        src = o_buf.at[pl.ds(r * 192, 192), :]
        dst = a_buf.at[:, pl.ds(pl.multiple_of(home_head * HD, HD), HD)]
        return own, src, dst, dev(z, yy, xx, xh, home_core)

    def send_rows(r):
        for xx in (0, 1):
            own, src, dst, target = home(r, xx)

            @pl.when(own)
            def _():
                pltpu.make_async_copy(src, dst, o_r.at[home_head]).start()

            @pl.when(jnp.logical_not(own))
            def _():
                remote(src, dst, o_s.at[r * 2 + xx], o_r.at[home_head], target).start()

    @pl.when(active)
    def _():
        for j in range(8):
            ref = q_win.at[pl.ds(j * ROWS, ROWS), :]
            remote(ref, ref, q_r.at[j], q_r.at[j], partner).wait_recv()
        for i in range(4):
            halo(i).wait_recv()

    for s in range(3):
        @pl.when(active)
        def _():
            attend(s)
            for r in ((0,), (1,), (2, 3))[s]:
                send_rows(r)
        ring_step(s)

    for k in range(2):
        for yy in range(NY):
            rows = lax.broadcasted_iota(jnp.int32, (PADDED, 640), 0)
            cols = lax.broadcasted_iota(jnp.int32, (PADDED, 640), 1)
            hit = (rows < COLS) & (cols == rows + (2 * yy + k) * COLS)
            spread[pl.ds(k * 384 + yy * PADDED, PADDED), :] = jnp.where(hit, 1.0, 0.0).astype(jnp.bfloat16)

    ring_step(3)

    for a in range(LOCAL_HEADS):
        ref = a_buf.at[:, pl.ds(a * HD, HD)]
        remote(ref, ref, o_r.at[a], o_r.at[a], partner).wait_recv()

    def project(block):
        first = wa[pl.ds(block * 2, 2)].reshape(768, KA)
        second = wb[pl.ds(block * 2, 2)].reshape(768, KB)
        dims = (((1,), (1,)), ((), ()))
        return (lax.dot_general(a_buf[:, :KA], first, dims, preferred_element_type=jnp.float32)
                + lax.dot_general(a_buf[:, KA:], second, dims, preferred_element_type=jnp.float32))

    for k in (0, 1):
        part[k] = project(2 * k + 1 - core).astype(jnp.bfloat16)
        remote(part.at[k], c_in.at[k], c_s.at[k], c_r.at[k], partner).start()

    out_slot = xh * 2 + xl

    def scatter(kh, kl):
        src = summed.at[kh, pl.ds(kl * ROWS, ROWS), :]
        return remote(src, x_in.at[out_slot], x_s.at[kh * 2 + kl], x_r.at[out_slot],
                      dev(z, y, kl, kh, core))

    for k in (0, 1):
        own = project(2 * k + core)
        remote(part.at[k], c_in.at[k], c_s.at[k], c_r.at[k], partner).wait_recv()
        summed[k] = (own + c_in[k].astype(jnp.float32)).astype(jnp.bfloat16)
        for kl in (0, 1):
            here = (k == xh) & (kl == xl)

            @pl.when(here)
            def _():
                x_in[out_slot] = summed[k, pl.ds(kl * ROWS, ROWS), :]

            @pl.when(jnp.logical_not(here))
            def _():
                scatter(k, kl).start()

    for i in range(4):
        @pl.when(i != out_slot)
        def _():
            remote(x_in.at[i], x_in.at[i], x_r.at[i], x_r.at[i], partner).wait_recv()
    for half in (0, 1):
        total = None
        for i in range(4):
            kl = i % 2
            piece = jnp.dot(x_in[i, :, pl.ds(half * 384, 384)], spread[pl.ds(kl * 384, 384), :],
                            preferred_element_type=jnp.float32)
            total = piece if total is None else total + piece
        out_ref[:, pl.ds(half * 640, 640)] = total.astype(jnp.bfloat16)

    for a in range(LOCAL_HEADS):
        @pl.when(jnp.logical_not(selves[a]))
        def _():
            kv_src = kv_ref.at[:, :, pl.ds(a * HD, HD)]
            q_src = q_ref.at[:, pl.ds(a * HD, HD)]
            remote(kv_src, kv_src, p1_s.at[a], p1_s.at[a], partner).wait_send()
            remote(q_src, q_src, p1_s.at[LOCAL_HEADS + a], p1_s.at[LOCAL_HEADS + a], partner).wait_send()
    for i in range(14):
        ref = wa.at[z, y] if i < 7 else wb.at[z, y]
        remote(ref, ref, w1_s.at[i], w1_s.at[i], partner).wait_send()
        ring(i).wait_send()

    @pl.when(active)
    def _():
        for i in range(4):
            halo(i).wait_send()
        for r in range(4):
            for xx in (0, 1):
                own, src, dst, target = home(r, xx)

                @pl.when(jnp.logical_not(own))
                def _():
                    remote(src, dst, o_s.at[r * 2 + xx], o_s.at[r * 2 + xx], target).wait_send()
    for k in (0, 1):
        remote(part.at[k], c_in.at[k], c_s.at[k], c_r.at[k], partner).wait_send()
    for kh in (0, 1):
        for kl in (0, 1):
            @pl.when(jnp.logical_not((kh == xh) & (kl == xl)))
            def _():
                scatter(kh, kl).wait_send()


def on_device(queries, keys_values, out_weight):
    weight = jnp.pad(out_weight.T, ((0, PADDED - COLS), (0, 0)))
    bf16 = jnp.bfloat16
    vmem = pl.BlockSpec(memory_space=pltpu.VMEM)
    dma = pltpu.SemaphoreType.DMA
    return pl.pallas_call(
        on_core,
        out_shape=jax.ShapeDtypeStruct((ROWS, 1280), bf16),
        in_specs=[vmem] * 3,
        out_specs=vmem,
        scratch_shapes=[
            pltpu.VMEM((2, WINDOW, HD), bf16),
            pltpu.VMEM((UNIT, HD), bf16),
            pltpu.VMEM((UNIT, HD), bf16),
            pltpu.VMEM((SUB, KEYS), jnp.float32),
            pltpu.VMEM((192, 640), bf16),
            pltpu.VMEM((NZ, NY, PADDED, KA), bf16),
            pltpu.VMEM((NZ, NY, PADDED, KB), bf16),
            pltpu.VMEM((2, 192, 768), bf16),
            pltpu.VMEM((2, 192, 768), bf16),
            pltpu.VMEM((2, 192, 768), bf16),
            pltpu.VMEM((4, ROWS, 768), bf16),
            pltpu.VMEM((768, 640), bf16),
            dma((10,)), dma((8,)), dma((8,)), dma((4,)), dma((4,)),
            dma((14,)), dma((14,)), dma((14,)), dma((14,)),
            dma((8,)), dma((5,)), dma((2,)), dma((2,)), dma((4,)), dma((4,)),
        ],
        compiler_params=pltpu.CompilerParams(
            collective_id=0, has_side_effects=True, vmem_limit_bytes=48 * 2 ** 20),
        cost_estimate=pl.CostEstimate(flops=2 * 10 ** 9, bytes_accessed=10 ** 6, transcendentals=2 * 10 ** 6),
        name="band_block",
    )(queries, keys_values, weight)


def solution(mesh):
    in_specs = (P("frames", "heads"), P(None, "frames", "heads"), P("heads", "frames"))
    out_specs = P("frames", "heads")
    return jax.shard_map(
        on_device, mesh=mesh, in_specs=in_specs, out_specs=out_specs, check_vma=False
    )
```

```python
import jax
import jax.numpy as jnp
from jax import lax
from jax.experimental import pallas as pl
from jax.experimental.pallas import tpu as pltpu
from jax.sharding import PartitionSpec as P

HD = 128
TPF = 32
NY = 8
NZ = 8
LOCAL_HEADS = 5
ROWS = 96
UNIT = 768
WINDOW = 2816
SUB = 256
KEYS = 2304
COLS = 40
QUARTER = NY // 2
WROWS = 208
NEG = -1e30
LOGE = 1.4426950408889634
MESH = pl.DeviceIdType.MESH


def on_core(q_ref, kv_ref, w_ref, out_ref,
            kv_win, q_win, o_buf, scores, a_buf, w_own, wbuf, full, part, c_in, summed, x_in, spread,
            w_sem, p1_s, kv_r, q_r, h_s, h_r, w1_s, w1_r, w2_s, w2_r, o_s, o_r, f_s, c_s, c_r, x_s, x_r):
    frames = lax.axis_index("frames")
    heads = lax.axis_index("heads")
    xl = lax.rem(frames, 2)
    y = lax.rem(lax.div(frames, 2), NY)
    z = lax.div(frames, 2 * NY)
    xh = lax.div(heads, 2)
    core = lax.rem(heads, 2)
    par = lax.rem(y, 2)
    fourth = lax.div(y, 2)

    def dev(zz, yy, xx, hh, cc):
        return ((zz * NY + yy) * 2 + xx, hh * 2 + cc)

    def remote(src, dst, send, recv, device):
        return pltpu.make_async_remote_copy(
            src_ref=src, dst_ref=dst, send_sem=send, recv_sem=recv,
            device_id=device, device_id_type=MESH)

    own_copy = pltpu.make_async_copy(w_ref, w_own, w_sem)
    own_copy.start()

    mine = (y * 2 + xl) * 2 + core
    partner = dev(z, y, xl, xh, 1 - core)
    barrier = pltpu.get_barrier_semaphore()

    def greet(device):
        pl.semaphore_signal(barrier, inc=1, device_id=device, device_id_type=MESH)

    for k in range(1, 32):
        other = lax.rem(mine + k, 32)
        greet(dev(z, lax.div(other, 4), lax.rem(lax.div(other, 2), 2), xh, lax.rem(other, 2)))
    for k in range(1, NZ):
        greet(dev(lax.rem(z + k, NZ), y, xl, xh, core))
    for k in (1, NZ - 1):
        greet(dev(lax.rem(z + k, NZ), y, xl, xh, 1 - core))
    for k in range(8):
        greet(dev(z, y - par + k // 4, lax.rem(k // 2, 2), 1 - xh, k % 2))
    spread[...] = jnp.zeros_like(spread)
    for i in range(4):
        for yy in range(QUARTER):
            rows = lax.broadcasted_iota(jnp.int32, (32, 640), 0)
            cols = lax.broadcasted_iota(jnp.int32, (32, 640), 1)
            first = (4 * yy + i) * COLS
            hit = jnp.where(cols == rows + first, 1.0, 0.0).astype(jnp.bfloat16)
            rows, cols = rows[:16], cols[:16]
            tail = jnp.where(cols == lax.rem(rows, 8) + (first + 32), 1.0, 0.0).astype(jnp.bfloat16)
            for zz in (0, 1):
                spread[zz, i, pl.ds(yy * 32, 32), :] = hit
                spread[zz, i, pl.ds(128 + zz * 64 + yy * 16, 16), :] = tail

    own_copy.wait()

    def tails(k, other):
        low = w_own[32:40, k * HD:(k + 1) * HD].astype(jnp.float32)
        high = jnp.zeros_like(low) if other is None else w_own[32:40, other * HD:(other + 1) * HD].astype(jnp.float32)
        return jnp.concatenate([low, high], axis=0).astype(jnp.bfloat16)

    def heads_of(k):
        return w_own[0:32, k * HD:(k + 1) * HD]

    wbuf[z, fourth, 0:32] = heads_of(0)
    wbuf[z, fourth, 32:48] = tails(0, 1)
    wbuf[z, fourth, 48:80] = heads_of(1)
    wbuf[z, fourth, 80:112] = heads_of(2)
    wbuf[z, fourth, 112:128] = tails(2, 3)
    wbuf[z, fourth, 128:160] = heads_of(3)
    wbuf[z, fourth, 160:192] = heads_of(4)
    wbuf[z, fourth, 192:208] = tails(4, None)
    pl.semaphore_wait(barrier, 31 + 7 + 2 + 8)

    slot = lax.rem(y, 4) * 2 + xl
    dest_core = lax.div(y, 4)
    def to_heads(a):
        wanted = core * LOCAL_HEADS + a
        yd, xd = lax.div(lax.div(wanted, 2) * 8, 5), lax.rem(wanted, 2)
        own = (yd == y) & (xd == xl) & (dest_core == core)
        return own, dev(z, yd, xd, xh, dest_core)

    def send_kv(a):
        own, target = to_heads(a)
        src = kv_ref.at[:, :, pl.ds(a * HD, HD)]
        dst = kv_win.at[:, pl.ds(pl.multiple_of(1024 + slot * ROWS, 32), ROWS), :]

        @pl.when(own)
        def _():
            pltpu.make_async_copy(src, dst, kv_r.at[slot]).start()

        @pl.when(jnp.logical_not(own))
        def _():
            remote(src, dst, p1_s.at[a], kv_r.at[slot], target).start()

    def send_q(a):
        own, target = to_heads(a)
        src = q_ref.at[:, pl.ds(a * HD, HD)]
        dst = q_win.at[pl.ds(pl.multiple_of(slot * ROWS, 32), ROWS), :]

        @pl.when(own)
        def _():
            pltpu.make_async_copy(src, dst, q_r.at[slot]).start()

        @pl.when(jnp.logical_not(own))
        def _():
            remote(src, dst, p1_s.at[LOCAL_HEADS + a], q_r.at[slot], target).start()

    def first_step(k):
        ref = wbuf.at[z, fourth]
        return remote(ref, ref, w1_s.at[k - 1], w1_r.at[k - 1],
                      dev(z, lax.rem(y + 2 * k, NY), xl, xh, core))

    def send_w():
        for k in range(1, QUARTER):
            first_step(k).start()

    pair = lax.div(y * 5 + 7, 8)
    head = pair * 2 + xl
    active = (lax.div(pair * 8, 5) == y) & (pair < LOCAL_HEADS)
    unit = z * 2 + core

    def unit_dev(shift):
        other = lax.rem(unit + shift + 16, 16)
        return dev(lax.div(other, 2), y, xl, xh, lax.rem(other, 2))

    halos = tuple((1024 + 192 * r, 192, 256 + 192 * r, 1) for r in range(4))
    halos += tuple((1024 + 192 * r, 192, 1792 + 192 * r, -1) for r in range(4))
    halos += ((1536, 256, 0, 2), (1024, 256, 2560, -2))

    def halo(i):
        start, size, to, shift = halos[i]
        return remote(kv_win.at[:, pl.ds(start, size), :], kv_win.at[:, pl.ds(to, size), :],
                      h_s.at[i], h_r.at[i], unit_dev(shift))

    def send_halos():
        @pl.when(active)
        def _():
            for r in range(4):
                for j in (2 * r, 2 * r + 1):
                    ref = kv_win.at[:, pl.ds(1024 + j * ROWS, ROWS), :]
                    remote(ref, ref, kv_r.at[j], kv_r.at[j], partner).wait_recv()
                halo(r).start()
                halo(4 + r).start()
                if r == 1:
                    halo(9).start()
                elif r == 3:
                    halo(8).start()

    sign = 1 - 2 * core

    def way_of(i):
        return (i, sign) if i < 4 else (i - 4, -sign)

    def ring(i):
        t, way = way_of(i)
        ref = wbuf.at[lax.rem(z - way * t + 2 * NZ, NZ)]
        return remote(ref, ref, w2_s.at[i], w2_r.at[i],
                      dev(lax.rem(z + way + NZ, NZ), y, xl, xh, core))

    def ring_arrival(i):
        t, way = way_of(i)
        ref = wbuf.at[lax.rem(z - way * (t + 1) + 2 * NZ, NZ)]
        remote(ref, ref, w2_r.at[i], w2_r.at[i], partner).wait_recv()

    def start_rings():
        for k in range(1, QUARTER):
            ref = wbuf.at[z, lax.rem(fourth - k + QUARTER, QUARTER)]
            remote(ref, ref, w1_r.at[k - 1], w1_r.at[k - 1], partner).wait_recv()
        ring(0).start()
        ring(4).start()

    def ring_step(t):
        for first, last in ((0, 3), (4, 6)):
            i = first + t
            if i < last:
                ring_arrival(i)
                ring(i + 1).start()
            elif i == last:
                ring_arrival(i)

    def attend(s):
        queries = q_win[pl.ds(s * SUB, SUB), :]
        top = jnp.full((SUB, 256), NEG, jnp.float32)
        rows = lax.broadcasted_iota(jnp.int32, (SUB, 256), 0) // TPF
        cols = lax.broadcasted_iota(jnp.int32, (SUB, 256), 1) // TPF
        for n in range(KEYS // 256):
            keys = kv_win[0, pl.ds(s * SUB + n * 256, 256), :]
            block = lax.dot_general(queries, keys, (((1,), (1,)), ((), ())),
                                    preferred_element_type=jnp.float32)
            if n == 0:
                block = jnp.where(cols >= rows, block, NEG)
            elif n == KEYS // 256 - 1:
                block = jnp.where(cols <= rows, block, NEG)
            scores[:, pl.ds(n * 256, 256)] = block
            top = jnp.maximum(top, block)
        peak = jnp.max(top, axis=1, keepdims=True)
        total = jnp.zeros((SUB, 256), jnp.float32)
        acc = jnp.zeros((SUB, HD), jnp.float32)
        for n in range(KEYS // 256):
            weights = jnp.exp2((scores[:, pl.ds(n * 256, 256)] - peak) * (LOGE * HD ** -0.5))
            total = total + weights
            values = kv_win[1, pl.ds(s * SUB + n * 256, 256), :]
            acc = acc + jnp.dot(weights.astype(jnp.bfloat16), values,
                                preferred_element_type=jnp.float32)
        norm = jnp.sum(total, axis=1, keepdims=True)
        o_buf[pl.ds(s * SUB, SUB), :] = (acc / norm).astype(jnp.bfloat16)

    home_core = lax.div(head, LOCAL_HEADS)
    home_head = lax.rem(head, LOCAL_HEADS)

    def home(r, i):
        yy = core * 4 + r * 2 + i
        own = (yy == y) & (home_core == core)
        src = o_buf.at[pl.ds(r * 384, 384), :]
        dst = a_buf.at[:, pl.ds(pl.multiple_of(home_head * HD, HD), HD)]
        return own, src, dst, dev(z, yy, xl, xh, home_core)

    def send_rows(r):
        for i in (0, 1):
            own, src, dst, target = home(r, i)

            @pl.when(own)
            def _():
                pltpu.make_async_copy(src, dst, o_r.at[home_head]).start()

            @pl.when(jnp.logical_not(own))
            def _():
                remote(src, dst, o_s.at[r * 2 + i], o_r.at[home_head], target).start()

    def from_here(a):
        return lax.rem(core * LOCAL_HEADS + a, 2) == xl

    def hand_on(a):
        ref = a_buf.at[:, pl.ds(a * HD, HD)]
        return remote(ref, ref, f_s.at[a], o_r.at[a], dev(z, y, 1 - xl, xh, core))

    def hand_on_rows():
        for a in range(LOCAL_HEADS):
            @pl.when(from_here(a))
            def _():
                hand_on(a).wait_recv()
                hand_on(a).start()

    def wait_window():
        @pl.when(active)
        def _():
            for j in range(8):
                ref = q_win.at[pl.ds(j * ROWS, ROWS), :]
                remote(ref, ref, q_r.at[j], q_r.at[j], partner).wait_recv()
            for i in range(10):
                halo(i).wait_recv()

    def step(s):
        @pl.when(active)
        def _():
            attend(s)
            for r in ((), (0,), (1,))[s]:
                send_rows(r)

    def kv_sent():
        for a in range(LOCAL_HEADS):
            @pl.when(jnp.logical_not(to_heads(a)[0]))
            def _():
                kv_src = kv_ref.at[:, :, pl.ds(a * HD, HD)]
                remote(kv_src, kv_src, p1_s.at[a], p1_s.at[a], partner).wait_send()

    send_w()
    for a in range(LOCAL_HEADS):
        send_kv(a)
    start_rings()
    send_halos()
    for a in range(LOCAL_HEADS):
        send_q(a)
    ring_step(0)
    wait_window()
    for s in range(3):
        step(s)
    ring_step(1)
    hand_on_rows()
    ring_step(2)

    def wait_rows():
        for a in range(LOCAL_HEADS):
            @pl.when(jnp.logical_not(from_here(a)))
            def _():
                hand_on(a).wait_recv()

    def project(block):
        dims = (((1,), (1,)), ((), ()))

        def piece(start, size):
            return wbuf[pl.ds(block * 2, 2), :, start:start + size].reshape(2 * QUARTER * size, HD)

        main = jnp.concatenate([piece(start, 32) for start in (0, 48, 80, 128, 160)], axis=1)
        ends = [piece(start, 16) for start in (32, 112, 192)]
        a = [a_buf[:, k * HD:(k + 1) * HD] for k in range(LOCAL_HEADS)]
        left = lax.dot_general(a_buf[...], main, dims, preferred_element_type=jnp.float32)
        even = lax.dot_general(jnp.concatenate([a[0], a[2], a[4]], axis=1), jnp.concatenate(ends, axis=1),
                               dims, preferred_element_type=jnp.float32)
        odd = lax.dot_general(jnp.concatenate([a[1], a[3]], axis=1), jnp.concatenate(ends[:2], axis=1),
                              dims, preferred_element_type=jnp.float32)
        lanes = lax.broadcasted_iota(jnp.int32, even.shape, 1)
        return jnp.concatenate([left, jnp.where(lax.rem(lanes, 16) < 8, even, odd)], axis=1)

    half, odd = lax.div(z, 2), lax.rem(z, 2)
    blocks = [half, lax.rem(half + 3 + 2 * odd, 4), lax.rem(half + 1 + 2 * odd, 4), lax.rem(half + 2, 4)]
    out_slot = (par * 2 + xl) * 2 + xh

    def swap(s):
        return remote(part.at[s], c_in.at[s], c_s.at[s], c_r.at[s], partner)

    def scatter(s, kl):
        kh, kc = lax.div(blocks[s], 2), lax.rem(blocks[s], 2)
        here = (kh == xh) & (kc == core) & (core == par) & (kl == xl)
        src = summed.at[s, pl.ds(kl * ROWS, ROWS), :]
        return here, remote(src, x_in.at[out_slot], x_s.at[s * 2 + kl], x_r.at[out_slot],
                            dev(z, y - par + core, kl, kh, kc))

    def begin(s):
        full[s] = project(blocks[s])
        part[s] = full[s, pl.ds(pl.multiple_of((1 - core) * 192, 64), 192), :].astype(jnp.bfloat16)
        swap(s).start()

    def finish(s):
        swap(s).wait_recv()
        own = full[s, pl.ds(pl.multiple_of(core * 192, 64), 192), :]
        summed[s] = (own + c_in[s].astype(jnp.float32)).astype(jnp.bfloat16)
        for kl in (0, 1):
            here, copy = scatter(s, kl)

            @pl.when(here)
            def _():
                x_in[out_slot] = summed[s, pl.ds(kl * ROWS, ROWS), :]

            @pl.when(jnp.logical_not(here))
            def _():
                copy.start()

    wait_rows()
    begin(0)
    begin(1)
    finish(0)
    begin(2)
    finish(1)
    ring_step(3)
    begin(3)
    finish(2)
    finish(3)

    for i in range(8):
        @pl.when((i != out_slot) | (core != par))
        def _():
            remote(x_in.at[i], x_in.at[i], x_r.at[i], x_r.at[i], partner).wait_recv()
    for zz in (0, 1):
        total = None
        for i in range(4):
            rows = x_in[2 * i:2 * i + 2].reshape(2 * ROWS, 384)
            rows = jnp.concatenate([rows[:, zz * 128:(zz + 1) * 128], rows[:, 256:]], axis=1)
            piece = jnp.dot(rows, spread[zz, i], preferred_element_type=jnp.float32)
            total = piece if total is None else total + piece
        out_ref[:, pl.ds(zz * 640, 640)] = (total[:ROWS] + total[ROWS:]).astype(jnp.bfloat16)

    for a in range(LOCAL_HEADS):
        @pl.when(jnp.logical_not(to_heads(a)[0]))
        def _():
            q_src = q_ref.at[:, pl.ds(a * HD, HD)]
            remote(q_src, q_src, p1_s.at[LOCAL_HEADS + a], p1_s.at[LOCAL_HEADS + a], partner).wait_send()
    kv_sent()
    for k in range(1, QUARTER):
        first_step(k).wait_send()
    for i in range(7):
        ring(i).wait_send()

    @pl.when(active)
    def _():
        for i in range(10):
            halo(i).wait_send()
        for r in (0, 1):
            for k in (0, 1):
                own, src, dst, target = home(r, k)

                @pl.when(jnp.logical_not(own))
                def _():
                    remote(src, dst, o_s.at[r * 2 + k], o_s.at[r * 2 + k], target).wait_send()
    for a in range(LOCAL_HEADS):
        @pl.when(from_here(a))
        def _():
            hand_on(a).wait_send()
    for s in range(4):
        swap(s).wait_send()
        for kl in (0, 1):
            here, copy = scatter(s, kl)

            @pl.when(jnp.logical_not(here))
            def _():
                copy.wait_send()


def on_device(queries, keys_values, out_weight):
    bf16 = jnp.bfloat16
    vmem = pl.BlockSpec(memory_space=pltpu.VMEM)
    dma = pltpu.SemaphoreType.DMA
    return pl.pallas_call(
        on_core,
        out_shape=jax.ShapeDtypeStruct((ROWS, 1280), bf16),
        in_specs=[pl.BlockSpec(memory_space=pl.ANY)] * 3,
        out_specs=vmem,
        scratch_shapes=[
            pltpu.VMEM((2, WINDOW, HD), bf16),
            pltpu.VMEM((UNIT, HD), bf16),
            pltpu.VMEM((UNIT, HD), bf16),
            pltpu.VMEM((SUB, KEYS), jnp.float32),
            pltpu.VMEM((384, 640), bf16),
            pltpu.VMEM((COLS, 640), bf16),
            pltpu.VMEM((NZ, QUARTER, WROWS, HD), bf16),
            pltpu.VMEM((4, 384, 384), jnp.float32),
            pltpu.VMEM((4, 192, 384), bf16),
            pltpu.VMEM((4, 192, 384), bf16),
            pltpu.VMEM((4, 192, 384), bf16),
            pltpu.VMEM((8, ROWS, 384), bf16),
            pltpu.VMEM((2, 4, 256, 640), bf16),
            dma, dma((10,)), dma((8,)), dma((8,)), dma((10,)), dma((10,)),
            dma((3,)), dma((3,)), dma((7,)), dma((7,)),
            dma((4,)), dma((5,)), dma((5,)), dma((4,)), dma((4,)), dma((8,)), dma((8,)),
        ],
        compiler_params=pltpu.CompilerParams(
            collective_id=0, has_side_effects=True, vmem_limit_bytes=62 * 2 ** 20),
        cost_estimate=pl.CostEstimate(flops=2 * 10 ** 9, bytes_accessed=10 ** 6, transcendentals=2 * 10 ** 6),
        name="band_block",
    )(queries, keys_values, out_weight.T)


def solution(mesh):
    in_specs = (P("frames", "heads"), P(None, "frames", "heads"), P("heads", "frames"))
    out_specs = P("frames", "heads")
    return jax.shard_map(
        on_device, mesh=mesh, in_specs=in_specs, out_specs=out_specs, check_vma=False
    )
```

```python
import jax
import jax.numpy as jnp
from jax import lax
from jax.experimental import pallas as pl
from jax.experimental.pallas import tpu as pltpu
from jax.sharding import PartitionSpec as P

HD = 128
TPF = 32
NY = 8
NZ = 8
LOCAL_HEADS = 5
ROWS = 96
UNIT = 768
WINDOW = 2816
SUB = 256
KEYS = 2304
COLS = 40
QUARTER = NY // 2
WROWS = 208
NEG = -1e30
LOGE = 1.4426950408889634
MESH = pl.DeviceIdType.MESH


def on_core(q_ref, kv_ref, w_ref, out_ref,
            kv_win, q_win, o_buf, scores, a_buf, w_own, wbuf, full, part, c_in, summed, x_in, spread,
            w_sem, p1_s, kv_r, q_r, h_s, h_r, w1_s, w1_r, w2_s, w2_r, o_s, o_r, f_s, c_s, c_r, x_s, x_r):
    frames = lax.axis_index("frames")
    heads = lax.axis_index("heads")
    xl = lax.rem(frames, 2)
    y = lax.rem(lax.div(frames, 2), NY)
    z = lax.div(frames, 2 * NY)
    xh = lax.div(heads, 2)
    core = lax.rem(heads, 2)
    par = lax.rem(y, 2)
    fourth = lax.div(y, 2)

    def dev(zz, yy, xx, hh, cc):
        return ((zz * NY + yy) * 2 + xx, hh * 2 + cc)

    def remote(src, dst, send, recv, device):
        return pltpu.make_async_remote_copy(
            src_ref=src, dst_ref=dst, send_sem=send, recv_sem=recv,
            device_id=device, device_id_type=MESH)

    own_copy = pltpu.make_async_copy(w_ref, w_own, w_sem)
    own_copy.start()

    mine = (y * 2 + xl) * 2 + core
    partner = dev(z, y, xl, xh, 1 - core)
    barrier = pltpu.get_barrier_semaphore()

    def greet(device):
        pl.semaphore_signal(barrier, inc=1, device_id=device, device_id_type=MESH)

    for k in range(1, 32):
        other = lax.rem(mine + k, 32)
        greet(dev(z, lax.div(other, 4), lax.rem(lax.div(other, 2), 2), xh, lax.rem(other, 2)))
    for k in range(1, NZ):
        greet(dev(lax.rem(z + k, NZ), y, xl, xh, core))
    for k in (1, NZ - 1):
        greet(dev(lax.rem(z + k, NZ), y, xl, xh, 1 - core))
    for k in range(8):
        greet(dev(z, y - par + k // 4, lax.rem(k // 2, 2), 1 - xh, k % 2))
    spread[...] = jnp.zeros_like(spread)
    for i in range(4):
        for yy in range(QUARTER):
            rows = lax.broadcasted_iota(jnp.int32, (32, 640), 0)
            cols = lax.broadcasted_iota(jnp.int32, (32, 640), 1)
            first = (4 * yy + i) * COLS
            hit = jnp.where(cols == rows + first, 1.0, 0.0).astype(jnp.bfloat16)
            rows, cols = rows[:16], cols[:16]
            tail = jnp.where(cols == lax.rem(rows, 8) + (first + 32), 1.0, 0.0).astype(jnp.bfloat16)
            for zz in (0, 1):
                spread[zz, i, pl.ds(yy * 32, 32), :] = hit
                spread[zz, i, pl.ds(128 + zz * 64 + yy * 16, 16), :] = tail

    own_copy.wait()

    def tails(k, other):
        low = w_own[32:40, k * HD:(k + 1) * HD].astype(jnp.float32)
        high = jnp.zeros_like(low) if other is None else w_own[32:40, other * HD:(other + 1) * HD].astype(jnp.float32)
        return jnp.concatenate([low, high], axis=0).astype(jnp.bfloat16)

    def heads_of(k):
        return w_own[0:32, k * HD:(k + 1) * HD]

    wbuf[z, fourth, 0:32] = heads_of(0)
    wbuf[z, fourth, 32:48] = tails(0, 1)
    wbuf[z, fourth, 48:80] = heads_of(1)
    wbuf[z, fourth, 80:112] = heads_of(2)
    wbuf[z, fourth, 112:128] = tails(2, 3)
    wbuf[z, fourth, 128:160] = heads_of(3)
    wbuf[z, fourth, 160:192] = heads_of(4)
    wbuf[z, fourth, 192:208] = tails(4, None)
    pl.semaphore_wait(barrier, 31 + 7 + 2 + 8)

    slot = lax.rem(y, 4) * 2 + xl
    dest_core = lax.div(y, 4)
    def to_heads(a):
        wanted = core * LOCAL_HEADS + a
        yd, xd = lax.div(lax.div(wanted, 2) * 8, 5), lax.rem(wanted, 2)
        own = (yd == y) & (xd == xl) & (dest_core == core)
        return own, dev(z, yd, xd, xh, dest_core)

    def send_kv(a):
        own, target = to_heads(a)
        src = kv_ref.at[:, :, pl.ds(a * HD, HD)]
        dst = kv_win.at[:, pl.ds(pl.multiple_of(1024 + slot * ROWS, 32), ROWS), :]

        @pl.when(own)
        def _():
            pltpu.make_async_copy(src, dst, kv_r.at[slot]).start()

        @pl.when(jnp.logical_not(own))
        def _():
            remote(src, dst, p1_s.at[a], kv_r.at[slot], target).start()

    def send_q(a):
        own, target = to_heads(a)
        src = q_ref.at[:, pl.ds(a * HD, HD)]
        dst = q_win.at[pl.ds(pl.multiple_of(slot * ROWS, 32), ROWS), :]

        @pl.when(own)
        def _():
            pltpu.make_async_copy(src, dst, q_r.at[slot]).start()

        @pl.when(jnp.logical_not(own))
        def _():
            remote(src, dst, p1_s.at[LOCAL_HEADS + a], q_r.at[slot], target).start()

    def first_step(k):
        ref = wbuf.at[z, fourth]
        return remote(ref, ref, w1_s.at[k - 1], w1_r.at[k - 1],
                      dev(z, lax.rem(y + 2 * k, NY), xl, xh, core))

    def send_w():
        for k in range(1, QUARTER):
            first_step(k).start()

    pair = lax.div(y * 5 + 7, 8)
    head = pair * 2 + xl
    active = (lax.div(pair * 8, 5) == y) & (pair < LOCAL_HEADS)
    unit = z * 2 + core

    def unit_dev(shift):
        other = lax.rem(unit + shift + 16, 16)
        return dev(lax.div(other, 2), y, xl, xh, lax.rem(other, 2))

    halos = tuple((1024 + 192 * r, 192, 256 + 192 * r, 1) for r in range(4))
    halos += tuple((1024 + 192 * r, 192, 1792 + 192 * r, -1) for r in range(4))
    halos += ((1536, 256, 0, 2), (1024, 256, 2560, -2))

    def halo(i):
        start, size, to, shift = halos[i]
        return remote(kv_win.at[:, pl.ds(start, size), :], kv_win.at[:, pl.ds(to, size), :],
                      h_s.at[i], h_r.at[i], unit_dev(shift))

    def send_halos():
        @pl.when(active)
        def _():
            for r in range(4):
                for j in (2 * r, 2 * r + 1):
                    ref = kv_win.at[:, pl.ds(1024 + j * ROWS, ROWS), :]
                    remote(ref, ref, kv_r.at[j], kv_r.at[j], partner).wait_recv()
                halo(r).start()
                halo(4 + r).start()
                if r == 1:
                    halo(9).start()
                elif r == 3:
                    halo(8).start()

    sign = 1 - 2 * core

    def way_of(i):
        return (i, sign) if i < 4 else (i - 4, -sign)

    def ring(i):
        t, way = way_of(i)
        ref = wbuf.at[lax.rem(z - way * t + 2 * NZ, NZ)]
        return remote(ref, ref, w2_s.at[i], w2_r.at[i],
                      dev(lax.rem(z + way + NZ, NZ), y, xl, xh, core))

    def ring_arrival(i):
        t, way = way_of(i)
        ref = wbuf.at[lax.rem(z - way * (t + 1) + 2 * NZ, NZ)]
        remote(ref, ref, w2_r.at[i], w2_r.at[i], partner).wait_recv()

    def start_rings():
        for k in range(1, QUARTER):
            ref = wbuf.at[z, lax.rem(fourth - k + QUARTER, QUARTER)]
            remote(ref, ref, w1_r.at[k - 1], w1_r.at[k - 1], partner).wait_recv()
        ring(0).start()
        ring(4).start()

    def ring_step(t):
        for first, last in ((0, 3), (4, 6)):
            i = first + t
            if i < last:
                ring_arrival(i)
                ring(i + 1).start()
            elif i == last:
                ring_arrival(i)

    def attend(s):
        queries = q_win[pl.ds(s * SUB, SUB), :]
        top = jnp.full((SUB, 256), NEG, jnp.float32)
        rows = lax.broadcasted_iota(jnp.int32, (SUB, 256), 0) // TPF
        cols = lax.broadcasted_iota(jnp.int32, (SUB, 256), 1) // TPF
        for n in range(KEYS // 256):
            keys = kv_win[0, pl.ds(s * SUB + n * 256, 256), :]
            block = lax.dot_general(queries, keys, (((1,), (1,)), ((), ())),
                                    preferred_element_type=jnp.float32)
            if n == 0:
                block = jnp.where(cols >= rows, block, NEG)
            elif n == KEYS // 256 - 1:
                block = jnp.where(cols <= rows, block, NEG)
            scores[:, pl.ds(n * 256, 256)] = block
            top = jnp.maximum(top, block)
        peak = jnp.max(top, axis=1, keepdims=True)
        total = jnp.zeros((SUB, 256), jnp.float32)
        acc = jnp.zeros((SUB, HD), jnp.float32)
        for n in range(KEYS // 256):
            weights = jnp.exp2((scores[:, pl.ds(n * 256, 256)] - peak) * (LOGE * HD ** -0.5))
            total = total + weights
            values = kv_win[1, pl.ds(s * SUB + n * 256, 256), :]
            acc = acc + jnp.dot(weights.astype(jnp.bfloat16), values,
                                preferred_element_type=jnp.float32)
        norm = jnp.sum(total, axis=1, keepdims=True)
        o_buf[pl.ds(s * SUB, SUB), :] = (acc / norm).astype(jnp.bfloat16)

    home_core = lax.div(head, LOCAL_HEADS)
    home_head = lax.rem(head, LOCAL_HEADS)

    def home(r, i):
        yy = core * 4 + r * 2 + i
        own = (yy == y) & (home_core == core)
        src = o_buf.at[pl.ds(r * 384, 384), :]
        dst = a_buf.at[:, pl.ds(pl.multiple_of(home_head * HD, HD), HD)]
        return own, src, dst, dev(z, yy, xl, xh, home_core)

    def send_rows(r):
        for i in (0, 1):
            own, src, dst, target = home(r, i)

            @pl.when(own)
            def _():
                pltpu.make_async_copy(src, dst, o_r.at[home_head]).start()

            @pl.when(jnp.logical_not(own))
            def _():
                remote(src, dst, o_s.at[r * 2 + i], o_r.at[home_head], target).start()

    def from_here(a):
        return lax.rem(core * LOCAL_HEADS + a, 2) == xl

    def hand_on(a):
        ref = a_buf.at[:, pl.ds(a * HD, HD)]
        return remote(ref, ref, f_s.at[a], o_r.at[a], dev(z, y, 1 - xl, xh, core))

    def hand_on_rows():
        for a in range(LOCAL_HEADS):
            @pl.when(from_here(a))
            def _():
                hand_on(a).wait_recv()
                hand_on(a).start()

    def wait_window():
        @pl.when(active)
        def _():
            for j in range(8):
                ref = q_win.at[pl.ds(j * ROWS, ROWS), :]
                remote(ref, ref, q_r.at[j], q_r.at[j], partner).wait_recv()
            for i in range(10):
                halo(i).wait_recv()

    def step(s):
        @pl.when(active)
        def _():
            attend(s)
            for r in ((), (0,), (1,))[s]:
                send_rows(r)

    def kv_sent():
        for a in range(LOCAL_HEADS):
            @pl.when(jnp.logical_not(to_heads(a)[0]))
            def _():
                kv_src = kv_ref.at[:, :, pl.ds(a * HD, HD)]
                remote(kv_src, kv_src, p1_s.at[a], p1_s.at[a], partner).wait_send()

    send_w()
    for a in range(LOCAL_HEADS):
        send_kv(a)
    start_rings()
    send_halos()
    for a in range(LOCAL_HEADS):
        send_q(a)
    wait_window()
    ring_step(0)
    for s in range(3):
        step(s)
    ring_step(1)
    hand_on_rows()
    ring_step(2)

    def wait_rows():
        for a in range(LOCAL_HEADS):
            @pl.when(jnp.logical_not(from_here(a)))
            def _():
                hand_on(a).wait_recv()

    def project(block):
        dims = (((1,), (1,)), ((), ()))

        def piece(start, size):
            return wbuf[pl.ds(block * 2, 2), :, start:start + size].reshape(2 * QUARTER * size, HD)

        main = jnp.concatenate([piece(start, 32) for start in (0, 48, 80, 128, 160)], axis=1)
        ends = [piece(start, 16) for start in (32, 112, 192)]
        a = [a_buf[:, k * HD:(k + 1) * HD] for k in range(LOCAL_HEADS)]
        left = lax.dot_general(a_buf[...], main, dims, preferred_element_type=jnp.float32)
        even = lax.dot_general(jnp.concatenate([a[0], a[2], a[4]], axis=1), jnp.concatenate(ends, axis=1),
                               dims, preferred_element_type=jnp.float32)
        odd = lax.dot_general(jnp.concatenate([a[1], a[3]], axis=1), jnp.concatenate(ends[:2], axis=1),
                              dims, preferred_element_type=jnp.float32)
        lanes = lax.broadcasted_iota(jnp.int32, even.shape, 1)
        return jnp.concatenate([left, jnp.where(lax.rem(lanes, 16) < 8, even, odd)], axis=1)

    half, odd = lax.div(z, 2), lax.rem(z, 2)
    blocks = [half, lax.rem(half + 3 + 2 * odd, 4), lax.rem(half + 1 + 2 * odd, 4), lax.rem(half + 2, 4)]
    out_slot = (par * 2 + xl) * 2 + xh

    def swap(s):
        return remote(part.at[s], c_in.at[s], c_s.at[s], c_r.at[s], partner)

    def scatter(s, kl):
        kh, kc = lax.div(blocks[s], 2), lax.rem(blocks[s], 2)
        here = (kh == xh) & (kc == core) & (core == par) & (kl == xl)
        src = summed.at[s, pl.ds(kl * ROWS, ROWS), :]
        return here, remote(src, x_in.at[out_slot], x_s.at[s * 2 + kl], x_r.at[out_slot],
                            dev(z, y - par + core, kl, kh, kc))

    def begin(s):
        full[s] = project(blocks[s])
        part[s] = full[s, pl.ds(pl.multiple_of((1 - core) * 192, 64), 192), :].astype(jnp.bfloat16)
        swap(s).start()

    def finish(s):
        swap(s).wait_recv()
        own = full[s, pl.ds(pl.multiple_of(core * 192, 64), 192), :]
        summed[s] = (own + c_in[s].astype(jnp.float32)).astype(jnp.bfloat16)
        for kl in (0, 1):
            here, copy = scatter(s, kl)

            @pl.when(here)
            def _():
                x_in[out_slot] = summed[s, pl.ds(kl * ROWS, ROWS), :]

            @pl.when(jnp.logical_not(here))
            def _():
                copy.start()

    wait_rows()
    begin(0)
    begin(1)
    finish(0)
    begin(2)
    finish(1)
    ring_step(3)
    begin(3)
    finish(2)
    finish(3)

    for i in range(8):
        @pl.when((i != out_slot) | (core != par))
        def _():
            remote(x_in.at[i], x_in.at[i], x_r.at[i], x_r.at[i], partner).wait_recv()
    for zz in (0, 1):
        total = None
        for i in range(4):
            rows = x_in[2 * i:2 * i + 2].reshape(2 * ROWS, 384)
            rows = jnp.concatenate([rows[:, zz * 128:(zz + 1) * 128], rows[:, 256:]], axis=1)
            piece = jnp.dot(rows, spread[zz, i], preferred_element_type=jnp.float32)
            total = piece if total is None else total + piece
        out_ref[:, pl.ds(zz * 640, 640)] = (total[:ROWS] + total[ROWS:]).astype(jnp.bfloat16)

    for a in range(LOCAL_HEADS):
        @pl.when(jnp.logical_not(to_heads(a)[0]))
        def _():
            q_src = q_ref.at[:, pl.ds(a * HD, HD)]
            remote(q_src, q_src, p1_s.at[LOCAL_HEADS + a], p1_s.at[LOCAL_HEADS + a], partner).wait_send()
    kv_sent()
    for k in range(1, QUARTER):
        first_step(k).wait_send()
    for i in range(7):
        ring(i).wait_send()

    @pl.when(active)
    def _():
        for i in range(10):
            halo(i).wait_send()
        for r in (0, 1):
            for k in (0, 1):
                own, src, dst, target = home(r, k)

                @pl.when(jnp.logical_not(own))
                def _():
                    remote(src, dst, o_s.at[r * 2 + k], o_s.at[r * 2 + k], target).wait_send()
    for a in range(LOCAL_HEADS):
        @pl.when(from_here(a))
        def _():
            hand_on(a).wait_send()
    for s in range(4):
        swap(s).wait_send()
        for kl in (0, 1):
            here, copy = scatter(s, kl)

            @pl.when(jnp.logical_not(here))
            def _():
                copy.wait_send()


def on_device(queries, keys_values, out_weight):
    bf16 = jnp.bfloat16
    vmem = pl.BlockSpec(memory_space=pltpu.VMEM)
    dma = pltpu.SemaphoreType.DMA
    return pl.pallas_call(
        on_core,
        out_shape=jax.ShapeDtypeStruct((ROWS, 1280), bf16),
        in_specs=[pl.BlockSpec(memory_space=pl.ANY)] * 3,
        out_specs=vmem,
        scratch_shapes=[
            pltpu.VMEM((2, WINDOW, HD), bf16),
            pltpu.VMEM((UNIT, HD), bf16),
            pltpu.VMEM((UNIT, HD), bf16),
            pltpu.VMEM((SUB, KEYS), jnp.float32),
            pltpu.VMEM((384, 640), bf16),
            pltpu.VMEM((COLS, 640), bf16),
            pltpu.VMEM((NZ, QUARTER, WROWS, HD), bf16),
            pltpu.VMEM((4, 384, 384), jnp.float32),
            pltpu.VMEM((4, 192, 384), bf16),
            pltpu.VMEM((4, 192, 384), bf16),
            pltpu.VMEM((4, 192, 384), bf16),
            pltpu.VMEM((8, ROWS, 384), bf16),
            pltpu.VMEM((2, 4, 256, 640), bf16),
            dma, dma((10,)), dma((8,)), dma((8,)), dma((10,)), dma((10,)),
            dma((3,)), dma((3,)), dma((7,)), dma((7,)),
            dma((4,)), dma((5,)), dma((5,)), dma((4,)), dma((4,)), dma((8,)), dma((8,)),
        ],
        compiler_params=pltpu.CompilerParams(
            collective_id=0, has_side_effects=True, vmem_limit_bytes=62 * 2 ** 20),
        cost_estimate=pl.CostEstimate(flops=2 * 10 ** 9, bytes_accessed=10 ** 6, transcendentals=2 * 10 ** 6),
        name="band_block",
    )(queries, keys_values, out_weight.T)


def solution(mesh):
    in_specs = (P("frames", "heads"), P(None, "frames", "heads"), P("heads", "frames"))
    out_specs = P("frames", "heads")
    return jax.shard_map(
        on_device, mesh=mesh, in_specs=in_specs, out_specs=out_specs, check_vma=False
    )
```
